32 devices in a mesh: row: 4 (over z), col: 8 (over y, x, core).
Axes of the slice: x: 2, y: 2, z: 4, core: 2. Of those that a mesh axis runs over, the one named last changes fastest.
Arguments:
- joined_weight: bfloat16 [8, 2880, 5760], P('row', 'col'), may hold values from -0.109375 to 0.109375
- tile_perm: int32 [144], replicated, may hold values from 0 to 143, each once
- down_weight: bfloat16 [8, 2880, 2880], P('row', 'col'), may hold values from -0.109375 to 0.109375
- tokens: bfloat16 [256, 2880], P(('row', 'col')), may hold values from -6 to 6
- expert_ids: int32 [256, 4], replicated, may hold values from 0 to 7, all different within a row; in each aligned block of 256 rows (0 to 255, 256 to 511, ...) at most 256 rows name the same one
- route_scores: float32 [256, 4], replicated, may hold values from 0.1 to 1
Outputs:
- gate_weight: bfloat16 [8, 2880, 2880], P('row', None, 'col')
- up_weight: bfloat16 [8, 2880, 2880], P('row', None, 'col')
- mixed: bfloat16 [256, 2880], P(('row', 'col'))
The draws below stay inside these ranges and needn't reach their ends.
Inputs may be any that keep to these rules, and one draw needn't show every extreme that they name: `expert_ids`: every expert is chosen by at most 256 tokens, a bound that some block reaches.
All inputs are finite; a program needn't handle non-finite values.
Results may differ from the reference program's by a relative error of at most 0.0049.
Values may be sent and summed in bfloat16 or wider, within the bound.
A program may use at most 128 MiB of HBM per device.

```python
import math
import jax
import jax.numpy as jnp
import numpy as np
from jax import lax

D = 2880
FF = 2880
TOP = 4
EXPERTS = 8
TOKENS = 256
TILES = 144
CAP = 256


def steps_of(own_key, extent, shards, smallest, top_value):
    factor_of, own = 1.0, jax.random.fold_in(own_key, 6)
    for axis_at, shards_of in shards:
        draws = jnp.exp(jax.random.uniform(jax.random.fold_in(own, axis_at), (shards_of,), jnp.float32, smallest / len(shards), top_value / len(shards)))
        factor_of = factor_of * jnp.repeat(draws, extent[axis_at] // shards_of).reshape([-1 if axis == axis_at else 1 for axis in range(len(extent))])
    return factor_of


def routed_block(key, own, number, rows, amount, top, most, lean):
    sequence = jax.random.permutation(key, amount)
    crowded, ordinary = load_shares(amount, rows * top, most, lean, True), load_shares(amount, rows * top, most, lean, False)
    places = jnp.arange(amount)

    def named(lengths, offset_by):
        used = int((lengths > 0).sum())
        fixed = max(1, used // 4)
        moved = fixed + (places - fixed + offset_by * (used - fixed)) % max(1, amount - fixed)
        return jnp.zeros((amount,), jnp.int32).at[sequence[jnp.where(places < fixed, places, moved)]].set(jnp.asarray(lengths, jnp.int32))

    lengths = jnp.where(number % 4 == 0, named(crowded, number // 4), named(ordinary, number - number // 4 - 1))
    mixed = jax.random.permutation(jax.random.fold_in(own, 3), amount)
    donor, receiver = mixed[0:amount // 2 * 2:2], mixed[1:amount // 2 * 2:2]
    room = jnp.minimum(lengths[donor] - 1, most - lengths[receiver]) // 2
    room = jnp.where((donor == sequence[0]) | (receiver == sequence[0]) | (lengths[receiver] == 0), 0, jnp.maximum(room, 0))
    moved = jax.random.randint(jax.random.fold_in(own, 4), (amount // 2,), 0, 1 << 20) % (room + 1)
    lengths = lengths.at[donor].add(-moved).at[receiver].add(moved)
    members = jnp.searchsorted(jnp.cumsum(lengths), jnp.arange(rows * top), side="right").astype(jnp.int32)
    grid = members.reshape(top, rows).T
    grid = grid[jax.random.permutation(jax.random.fold_in(own, 1), rows)]
    offset_by = jax.random.randint(jax.random.fold_in(own, 2), (rows, 1), 0, top)
    return jnp.take_along_axis(grid, (jnp.arange(top)[None, :] + offset_by) % top, axis=1)


def load_shares(count, total, reach, slope, full):
    loads = [(1 << 20) // math.isqrt(standing ** slope) + 1 for standing in range(1, count + 1)]
    largest = reach if full else min(reach, max(-(-total // count), total * loads[0] // sum(loads)))
    least = 1 if total - largest >= count - 1 else 0
    given, spare = [largest] + [least] * (count - 1), total - largest - least * (count - 1)
    while spare > 0:
        free = [i for i in range(1, count) if given[i] < largest] or [i for i in range(1, count) if given[i] < reach]
        mass, remaining = sum([loads[i] for i in free]), spare
        for i in free:
            more = min(reach - given[i], max(1, remaining * loads[i] // mass), spare)
            given[i] = given[i] + more
            spare = spare - more
    return np.array(given)


def scatter_about(key, extent, deviation, most, shards=(), held_as=jnp.bfloat16):
    loudness = steps_of(key, extent, shards, -0.22, 0.18) if shards else 1.0
    entries = jax.random.normal(key, extent, jnp.float32) * deviation * loudness
    return jnp.minimum(jnp.maximum(entries, -most), most).astype(held_as)


def setup_inputs(seed: int = 0) -> dict:
    arg_keys = jax.random.split(jax.random.key(seed), 7)
    joined_weight = scatter_about(arg_keys[0], (EXPERTS, D, 2 * FF), D ** -0.5, 0.109375, ((0, 4), (1, 8)))
    tile_perm = jax.random.permutation(arg_keys[1], TILES).astype(jnp.int32)
    down_weight = scatter_about(arg_keys[2], (EXPERTS, FF, D), FF ** -0.5, 0.109375, ((0, 4), (1, 8)))
    tokens = scatter_about(arg_keys[3], (TOKENS, D), 1.0, 6.0, ((0, 32),))
    expert_ids_keys = jax.random.split(jax.random.fold_in(arg_keys[4], 1), TOKENS // TOKENS)
    expert_ids_turns = jax.random.permutation(jax.random.fold_in(arg_keys[4], 3), TOKENS // TOKENS)
    expert_ids = jax.vmap(lambda own, number: routed_block(jax.random.fold_in(arg_keys[4], 2), own, number, TOKENS, EXPERTS, TOP, CAP, 0))(expert_ids_keys, expert_ids_turns).reshape((TOKENS, TOP))
    route_scores = jnp.clip(jnp.exp(jax.random.uniform(arg_keys[5], (TOKENS, TOP), jnp.float32, math.log(0.1), math.log(1.0))), 0.1, 1.0)
    return dict(joined_weight=joined_weight, tile_perm=tile_perm, down_weight=down_weight, tokens=tokens, expert_ids=expert_ids, route_scores=route_scores)


def reference(joined_weight, tile_perm, down_weight, tokens, expert_ids, route_scores):
    tiles = tile_perm.shape[0]
    width = joined_weight.shape[2]
    tile_cols = width // tiles
    inverse = jnp.argsort(tile_perm).astype(jnp.int32)
    logical = jnp.arange(width, dtype=jnp.int32)
    stored = inverse[logical // tile_cols] * tile_cols + logical % tile_cols
    ordered = jnp.take(joined_weight, stored, axis=2)
    gate_weight = ordered[:, :, 0::2]
    up_weight = ordered[:, :, 1::2]
    weights = route_scores / jnp.sum(route_scores, axis=1, keepdims=True)

    def add_expert(total, expert):
        share = jnp.sum(weights * (expert_ids == expert), axis=1)
        pre_gate = jnp.dot(tokens, gate_weight[expert], preferred_element_type=jnp.float32)
        pre_up = jnp.dot(tokens, up_weight[expert], preferred_element_type=jnp.float32)
        active = share[:, None] * (pre_up + 1.0) * pre_gate * jax.nn.sigmoid(1.702 * pre_gate)
        active = active.astype(jnp.bfloat16)
        return total + jnp.dot(active, down_weight[expert], preferred_element_type=jnp.float32), None

    start = jnp.zeros((tokens.shape[0], tokens.shape[1]), jnp.float32)
    total, unused = lax.scan(add_expert, start, jnp.arange(joined_weight.shape[0], dtype=jnp.int32))
    return gate_weight, up_weight, total.astype(jnp.bfloat16)
```

```python
import functools

import jax
import jax.numpy as jnp
import numpy as np
from jax import lax
from jax.experimental import pallas as pl
from jax.experimental.pallas import tpu as pltpu
from jax.sharding import PartitionSpec as P

MESH = pl.DeviceIdType.MESH
LANES = 128
WINDOW = 256


def partner_of(me, step, size):
    other = me
    bit = 1
    while bit < size:
        other = other + ((step // bit) % 2) * (1 - 2 * ((me // bit) % 2)) * bit
        bit *= 2
    return other


def block_plan(half, tile_cols):
    unit = tile_cols // 2
    plan, rows = [], []
    for first in range(0, half, LANES):
        units = first + np.arange(LANES)
        tiles = sorted(set((units[units < half] // unit).tolist()))
        at = []
        for tile in tiles:
            mine = (units // unit == tile) & (units < half)
            lane = np.where(mine, 2 * (units % unit), -(1 << 20))
            at.append(len(rows))
            rows.append(np.concatenate([lane, lane + 1]))
        plan.append((first, tiles, at))
    return plan, np.stack(rows).astype(np.int32)


def pack_kernel(n, plan, tiles_each, padded, start_ref, off_ref, lane_ref, joined_ref, recv_ref,
                held, send_buf, pick, send_sem, recv_sem, own_sem, load_sem):
    me, row = lax.axis_index("col"), lax.axis_index("row")
    local, blocks = joined_ref.shape[0], held.shape[0]

    def load_of(b):
        return pltpu.make_async_copy(
            joined_ref.at[:, :, b * LANES:(b + 1) * LANES], held.at[b], load_sem.at[b]
        )

    for b in range(blocks):
        load_of(b).start()
    barrier = pltpu.get_barrier_semaphore()
    for step in range(1, n):
        pl.semaphore_signal(barrier, inc=1, device_id=(row, partner_of(me, step, n)), device_id_type=MESH)
    pl.semaphore_wait(barrier, n - 1)

    def copy_of(turn, other):
        return pltpu.make_async_remote_copy(
            src_ref=send_buf.at[turn],
            dst_ref=recv_ref.at[me],
            send_sem=send_sem.at[turn],
            recv_sem=recv_sem.at[turn],
            device_id=(row, other),
            device_id_type=MESH,
        )

    def step_of(turn):
        return (n - 1) - (2 * turn) % (n - 1)

    def pack(turn, other):
        rows = lax.broadcasted_iota(jnp.int32, (WINDOW, 2 * LANES), 0)
        for first, tiles, at in plan:
            starts = []
            for k, tile in enumerate(tiles):
                starts.append(start_ref[other * tiles_each + tile])
                off = off_ref[other * tiles_each + tile]
                wanted = lane_ref[pl.ds(at[k], 1), :] + off
                pick[k * WINDOW:(k + 1) * WINDOW, :] = jnp.where(rows == wanted, 1.0, 0.0).astype(pick.dtype)
            depth = len(tiles) * WINDOW
            for e in range(local):
                x = jnp.concatenate([held[s + w, e] for s in starts for w in range(WINDOW // LANES)], axis=1)
                y = jnp.dot(x, pick[:depth, :], preferred_element_type=jnp.float32).astype(send_buf.dtype)
                send_buf[turn, e, :, first:first + LANES] = y[:, :LANES]
                send_buf[turn, e, :, padded + first:padded + first + LANES] = y[:, LANES:]

    def send(turn, carry):
        other = partner_of(me, step_of(turn), n)
        pack(turn, other)
        copy_of(turn, other).start()
        return carry

    for b in range(blocks):
        load_of(b).wait()
    lax.fori_loop(0, n - 1, send, 0)
    pack(n - 1, me)
    own = pltpu.make_async_copy(send_buf.at[n - 1], recv_ref.at[me], own_sem)
    own.start()

    def finish(turn, carry):
        copy_of(turn, partner_of(me, step_of(turn), n)).wait()
        return carry

    lax.fori_loop(0, n - 1, finish, 0)
    own.wait()


def exchange(joined_weight, start, off, n, half, tile_cols):
    local, rows, width = joined_weight.shape
    plan, lanes = block_plan(half, tile_cols)
    padded = len(plan) * LANES
    most = max(len(tiles) for _, tiles, _ in plan)
    smem = pl.BlockSpec(memory_space=pltpu.SMEM)
    vmem = pl.BlockSpec(memory_space=pltpu.VMEM)
    return pl.pallas_call(
        functools.partial(pack_kernel, n, plan, 2 * half // tile_cols, padded),
        out_shape=jax.ShapeDtypeStruct((n, local, rows, 2 * padded), joined_weight.dtype),
        in_specs=[smem, smem, vmem, pl.BlockSpec(memory_space=pl.ANY)],
        out_specs=pl.BlockSpec(memory_space=pl.ANY),
        scratch_shapes=[
            pltpu.VMEM((width // LANES, local, rows, LANES), joined_weight.dtype),
            pltpu.VMEM((n, local, rows, 2 * padded), joined_weight.dtype),
            pltpu.VMEM((most * WINDOW, 2 * LANES), joined_weight.dtype),
            pltpu.SemaphoreType.DMA((n - 1,)),
            pltpu.SemaphoreType.DMA((n - 1,)),
            pltpu.SemaphoreType.DMA,
            pltpu.SemaphoreType.DMA((width // LANES,)),
        ],
        compiler_params=pltpu.CompilerParams(
            collective_id=0, has_side_effects=True, vmem_limit_bytes=48 << 20
        ),
        cost_estimate=pl.CostEstimate(
            flops=2 * local * rows * WINDOW * 2 * width, bytes_accessed=4 * local * rows * width, transcendentals=0
        ),
        name="exchange",
    )(start, off, jnp.asarray(lanes), joined_weight)


def expert_kernel(n, padded, recv_ref, tok_ref, share_ref, down_ref, gate_ref, up_ref, part_ref, total):
    e, last = pl.program_id(0), pl.num_programs(0) - 1
    rows, half = recv_ref.shape[2], gate_ref.shape[2]
    for c in range(n):
        gate_ref[0, c * rows:(c + 1) * rows, :] = recv_ref[c, 0, :, :half]
        up_ref[0, c * rows:(c + 1) * rows, :] = recv_ref[c, 0, :, padded:padded + half]
    tokens = tok_ref[...]
    pre_gate = jnp.dot(tokens, gate_ref[0], preferred_element_type=jnp.float32)
    pre_up = jnp.dot(tokens, up_ref[0], preferred_element_type=jnp.float32)
    active = share_ref[0] * (pre_up + 1.0) * pre_gate * jax.nn.sigmoid(1.702 * pre_gate)
    active = active.astype(down_ref.dtype)
    depth = down_ref.shape[2]
    for first in range(0, depth, 512):
        cols = slice(first, min(depth, first + 512))
        term = jnp.dot(active, down_ref[0, :, cols], preferred_element_type=jnp.float32)

        @pl.when(e == 0)
        def _():
            total[:, cols] = term

        @pl.when(e > 0)
        def _():
            total[:, cols] += term

    @pl.when(e == last)
    def _():
        part_ref[...] = total[...].astype(part_ref.dtype)


def experts(recv, tokens, share, down_weight):
    n, local, rows, wide = recv.shape
    half, depth = down_weight.shape[1:]
    count = tokens.shape[0]
    dtype = recv.dtype
    return pl.pallas_call(
        functools.partial(expert_kernel, n, wide // 2),
        grid=(local,),
        out_shape=(
            jax.ShapeDtypeStruct((local, n * rows, half), dtype),
            jax.ShapeDtypeStruct((local, n * rows, half), dtype),
            jax.ShapeDtypeStruct((count, depth), dtype),
        ),
        in_specs=[
            pl.BlockSpec((n, 1, rows, wide), lambda e: (0, e, 0, 0)),
            pl.BlockSpec((count, depth), lambda e: (0, 0)),
            pl.BlockSpec((1, count, 1), lambda e: (e, 0, 0)),
            pl.BlockSpec((1, half, depth), lambda e: (e, 0, 0)),
        ],
        out_specs=(
            pl.BlockSpec((1, n * rows, half), lambda e: (e, 0, 0)),
            pl.BlockSpec((1, n * rows, half), lambda e: (e, 0, 0)),
            pl.BlockSpec((count, depth), lambda e: (0, 0)),
        ),
        scratch_shapes=[pltpu.VMEM((count, depth), jnp.float32)],
        compiler_params=pltpu.CompilerParams(
            dimension_semantics=("arbitrary",), vmem_limit_bytes=56 << 20
        ),
        name="experts",
    )(recv, tokens, share, down_weight)


def reduce_kernel(n, m, part_ref, out_ref, near, far, sums, held, near_send, near_recv, far_send, far_recv):
    me, row = lax.axis_index("col"), lax.axis_index("row")
    barrier = pltpu.get_barrier_semaphore()
    for step in range(1, n):
        pl.semaphore_signal(barrier, inc=1, device_id=(row, partner_of(me, step, n)), device_id_type=MESH)
    for step in range(1, m):
        pl.semaphore_signal(barrier, inc=1, device_id=(partner_of(row, step, m), me), device_id_type=MESH)
    pl.semaphore_wait(barrier, n + m - 2)
    slab = part_ref.shape[0] // n
    own = out_ref.shape[0]
    copies = []
    for step in range(n - 1, 0, -1):
        other = partner_of(me, step, n)
        copies.append(pltpu.make_async_remote_copy(
            src_ref=part_ref.at[pl.ds(pl.multiple_of(other * slab, slab), slab)],
            dst_ref=near.at[step - 1],
            send_sem=near_send.at[step - 1],
            recv_sem=near_recv.at[step - 1],
            device_id=(row, other),
            device_id_type=MESH,
        ))
        copies[-1].start()
    for copy in copies:
        copy.wait()
    total = part_ref[pl.ds(pl.multiple_of(me * slab, slab), slab), :].astype(jnp.float32)
    for step in range(1, n):
        total = total + near[step - 1].astype(jnp.float32)
    for r in range(m):
        sums[r] = total[r * own:(r + 1) * own, :]
        held[r] = total[r * own:(r + 1) * own, :].astype(held.dtype)
    copies = []
    for step in range(m - 1, 0, -1):
        other = partner_of(row, step, m)
        copies.append(pltpu.make_async_remote_copy(
            src_ref=held.at[other],
            dst_ref=far.at[step - 1],
            send_sem=far_send.at[step - 1],
            recv_sem=far_recv.at[step - 1],
            device_id=(other, me),
            device_id_type=MESH,
        ))
        copies[-1].start()
    for copy in copies:
        copy.wait()
    total = sums[row]
    for step in range(1, m):
        total = total + far[step - 1].astype(jnp.float32)
    out_ref[...] = total.astype(out_ref.dtype)


def reduce_scatter(part, n, m):
    count, depth = part.shape
    own = count // (n * m)
    vmem = pl.BlockSpec(memory_space=pltpu.VMEM)
    dma = pltpu.SemaphoreType.DMA
    return pl.pallas_call(
        functools.partial(reduce_kernel, n, m),
        out_shape=jax.ShapeDtypeStruct((own, depth), part.dtype),
        in_specs=[vmem],
        out_specs=vmem,
        scratch_shapes=[
            pltpu.VMEM((n - 1, count // n, depth), part.dtype),
            pltpu.VMEM((m - 1, own, depth), part.dtype),
            pltpu.VMEM((m, own, depth), jnp.float32),
            pltpu.VMEM((m, own, depth), part.dtype),
            dma((n - 1,)), dma((n - 1,)), dma((m - 1,)), dma((m - 1,)),
        ],
        compiler_params=pltpu.CompilerParams(
            collective_id=1, has_side_effects=True, vmem_limit_bytes=48 << 20
        ),
        name="reduce_scatter",
    )(part)


def body(joined_weight, tile_perm, down_weight, tokens, expert_ids, route_scores):
    n, m = lax.axis_size("col"), lax.axis_size("row")
    local, _, width = joined_weight.shape
    half = width // 2 // n
    tiles = tile_perm.shape[0]
    tile_cols = width // tiles
    places = jnp.arange(tiles, dtype=jnp.int32)
    inverse = jnp.sum(places[:, None] * (tile_perm[:, None] == places[None, :]), axis=0)
    first = inverse * tile_cols
    block = jnp.minimum(first // LANES, width // LANES - WINDOW // LANES)
    recv = exchange(joined_weight, block, first - block * LANES, n, half, tile_cols)
    everything = lax.all_gather(tokens, ("col", "row"), axis=0, tiled=True)
    expert_global = lax.axis_index("row") * local + jnp.arange(local, dtype=jnp.int32)
    weights = route_scores / jnp.sum(route_scores, axis=1, keepdims=True)
    share = jnp.sum(
        weights[None, :, :] * (expert_ids[None, :, :] == expert_global[:, None, None]), axis=2
    )
    own = tokens.shape[0]
    share = share.reshape(local, m, n, own).transpose(0, 2, 1, 3).reshape(local, -1, 1)
    gate, up, part = experts(recv, everything, share, down_weight)
    return gate, up, reduce_scatter(part, n, m)


def solution(mesh):
    placed = (P("row", "col", None), P(), P("row", "col", None), P(("row", "col"), None), P(), P())
    return jax.shard_map(
        body,
        mesh=mesh,
        in_specs=placed,
        out_specs=(P("row", None, "col"), P("row", None, "col"), P(("row", "col"), None)),
        check_vma=False,
    )
```

```python
import functools

import jax
import jax.numpy as jnp
import numpy as np
from jax import lax
from jax.experimental import pallas as pl
from jax.experimental.pallas import tpu as pltpu
from jax.sharding import PartitionSpec as P

MESH = pl.DeviceIdType.MESH
LANES = 128
WINDOW = 256
NT = (((1,), (1,)), ((), ()))


def partner_of(me, step, size):
    other = me
    bit = 1
    while bit < size:
        other = other + ((step // bit) % 2) * (1 - 2 * ((me // bit) % 2)) * bit
        bit *= 2
    return other


def block_plan(half, tile_cols):
    unit = tile_cols // 2
    plan, rows = [], []
    for first in range(0, half, LANES):
        units = first + np.arange(LANES)
        tiles = sorted(set((units[units < half] // unit).tolist()))
        at = []
        for tile in tiles:
            mine = (units // unit == tile) & (units < half)
            lane = np.where(mine, 2 * (units % unit), -(1 << 20))
            at.append(len(rows))
            rows.append(np.concatenate([lane, lane + 1]))
        plan.append((first, min(LANES, half - first), tiles, at))
    return plan, np.stack(rows, axis=1).astype(np.int32)


def pack_kernel(n, plan, tiles_each, start_ref, off_ref, lane_ref, joined_ref, recv_ref,
                held, send_buf, pick, send_sem, recv_sem, own_sem, load_sem):
    me, row = lax.axis_index("col"), lax.axis_index("row")
    local, blocks = joined_ref.shape[0], held.shape[0]

    def load_of(b):
        return pltpu.make_async_copy(
            joined_ref.at[:, :, b * LANES:(b + 1) * LANES], held.at[b], load_sem.at[b]
        )

    for b in range(blocks):
        load_of(b).start()
    barrier = pltpu.get_barrier_semaphore()
    for step in range(1, n):
        pl.semaphore_signal(barrier, inc=1, device_id=(row, partner_of(me, step, n)), device_id_type=MESH)
    pl.semaphore_wait(barrier, n - 1)

    def copy_of(turn, other):
        return pltpu.make_async_remote_copy(
            src_ref=send_buf.at[turn],
            dst_ref=recv_ref.at[me],
            send_sem=send_sem.at[turn],
            recv_sem=recv_sem.at[turn],
            device_id=(row, other),
            device_id_type=MESH,
        )

    def step_of(turn):
        return (n - 1) - (2 * turn) % (n - 1)

    def pack(turn, other):
        columns = lax.broadcasted_iota(jnp.int32, (2 * LANES, WINDOW), 1)
        for first, count, tiles, at in plan:
            starts = []
            for k, tile in enumerate(tiles):
                starts.append(start_ref[other * tiles_each + tile])
                off = off_ref[other * tiles_each + tile]
                wanted = lane_ref[:, at[k]:at[k] + 1] + off
                pick[:, k * WINDOW:(k + 1) * WINDOW] = jnp.where(columns == wanted, 1.0, 0.0).astype(pick.dtype)
            depth = len(tiles) * WINDOW
            for e in range(local):
                x = jnp.concatenate([held[s + w, e] for s in starts for w in range(WINDOW // LANES)], axis=1)
                y = lax.dot_general(pick[:, :depth], x, NT, preferred_element_type=jnp.float32)
                y = y.astype(send_buf.dtype)
                send_buf[turn, e, 0, first:first + count, :] = y[:count]
                send_buf[turn, e, 1, first:first + count, :] = y[LANES:LANES + count]

    def send(turn, carry):
        other = partner_of(me, step_of(turn), n)
        pack(turn, other)
        copy_of(turn, other).start()
        return carry

    for b in range(blocks):
        load_of(b).wait()
    lax.fori_loop(0, n - 1, send, 0)
    pack(n - 1, me)
    own = pltpu.make_async_copy(send_buf.at[n - 1], recv_ref.at[me], own_sem)
    own.start()

    def finish(turn, carry):
        copy_of(turn, partner_of(me, step_of(turn), n)).wait()
        return carry

    lax.fori_loop(0, n - 1, finish, 0)
    own.wait()


def exchange(joined_weight, start, off, n, half, tile_cols):
    local, rows, width = joined_weight.shape
    plan, lanes = block_plan(half, tile_cols)
    most = max(len(tiles) for _, _, tiles, _ in plan)
    smem = pl.BlockSpec(memory_space=pltpu.SMEM)
    vmem = pl.BlockSpec(memory_space=pltpu.VMEM)
    return pl.pallas_call(
        functools.partial(pack_kernel, n, plan, 2 * half // tile_cols),
        out_shape=jax.ShapeDtypeStruct((n, local, 2, half, rows), joined_weight.dtype),
        in_specs=[smem, smem, vmem, pl.BlockSpec(memory_space=pl.ANY)],
        out_specs=pl.BlockSpec(memory_space=pl.ANY),
        scratch_shapes=[
            pltpu.VMEM((width // LANES, local, rows, LANES), joined_weight.dtype),
            pltpu.VMEM((n, local, 2, half, rows), joined_weight.dtype),
            pltpu.VMEM((2 * LANES, most * WINDOW), joined_weight.dtype),
            pltpu.SemaphoreType.DMA((n - 1,)),
            pltpu.SemaphoreType.DMA((n - 1,)),
            pltpu.SemaphoreType.DMA,
            pltpu.SemaphoreType.DMA((width // LANES,)),
        ],
        compiler_params=pltpu.CompilerParams(
            collective_id=0, has_side_effects=True, vmem_limit_bytes=48 << 20
        ),
        cost_estimate=pl.CostEstimate(
            flops=2 * local * rows * WINDOW * 2 * width, bytes_accessed=4 * local * rows * width, transcendentals=0
        ),
        name="exchange",
    )(start, off, jnp.asarray(lanes), joined_weight)


def expert_kernel(n, base_ref, recv_ref, tok_ref, ids_ref, scores_ref, order_ref, down_ref,
                  gate_ref, up_ref, part_ref, total):
    e, last = pl.program_id(0), pl.num_programs(0) - 1
    rows = recv_ref.shape[4]
    for c in range(n):
        gate_ref[0, :, c * rows:(c + 1) * rows] = recv_ref[c, 0, 0]
        up_ref[0, :, c * rows:(c + 1) * rows] = recv_ref[c, 0, 1]
    scores = scores_ref[...]
    mine = jnp.where(ids_ref[...] == base_ref[0] + e, scores, 0.0)
    shares = jnp.sum(mine, axis=0, keepdims=True) / jnp.sum(scores, axis=0, keepdims=True)
    count = tok_ref.shape[0]
    source = lax.broadcasted_iota(jnp.int32, (count, count), 1)
    share = jnp.sum(jnp.where(source == order_ref[...], shares, 0.0), axis=1, keepdims=True)
    tokens = tok_ref[...]
    pre_gate = lax.dot_general(tokens, gate_ref[0], NT, preferred_element_type=jnp.float32)
    pre_up = lax.dot_general(tokens, up_ref[0], NT, preferred_element_type=jnp.float32)
    active = share * (pre_up + 1.0) * pre_gate * jax.nn.sigmoid(1.702 * pre_gate)
    active = active.astype(down_ref.dtype)
    depth = down_ref.shape[2]
    for first in range(0, depth, 512):
        cols = slice(first, min(depth, first + 512))
        term = jnp.dot(active, down_ref[0, :, cols], preferred_element_type=jnp.float32)

        @pl.when(e == 0)
        def _():
            total[:, cols] = term

        @pl.when(e > 0)
        def _():
            total[:, cols] += term

    @pl.when(e == last)
    def _():
        part_ref[...] = total[...].astype(part_ref.dtype)


def experts(base, recv, tokens, ids, scores, order, down_weight):
    n, local, _, _, rows = recv.shape
    half, depth = down_weight.shape[1:]
    count = tokens.shape[0]
    dtype = recv.dtype
    return pl.pallas_call(
        functools.partial(expert_kernel, n),
        grid=(local,),
        out_shape=(
            jax.ShapeDtypeStruct((local, half, n * rows), dtype),
            jax.ShapeDtypeStruct((local, half, n * rows), dtype),
            jax.ShapeDtypeStruct((count, depth), dtype),
        ),
        in_specs=[
            pl.BlockSpec(memory_space=pltpu.SMEM),
            pl.BlockSpec((n, 1, 2, half, rows), lambda e: (0, e, 0, 0, 0)),
            pl.BlockSpec((count, depth), lambda e: (0, 0)),
            pl.BlockSpec(ids.shape, lambda e: (0, 0)),
            pl.BlockSpec(scores.shape, lambda e: (0, 0)),
            pl.BlockSpec(order.shape, lambda e: (0, 0)),
            pl.BlockSpec((1, half, depth), lambda e: (e, 0, 0)),
        ],
        out_specs=(
            pl.BlockSpec((1, half, n * rows), lambda e: (e, 0, 0)),
            pl.BlockSpec((1, half, n * rows), lambda e: (e, 0, 0)),
            pl.BlockSpec((count, depth), lambda e: (0, 0)),
        ),
        scratch_shapes=[pltpu.VMEM((count, depth), jnp.float32)],
        compiler_params=pltpu.CompilerParams(
            dimension_semantics=("arbitrary",), vmem_limit_bytes=56 << 20
        ),
        name="experts",
    )(base, recv, tokens, ids, scores, order, down_weight)


def reduce_kernel(n, m, part_ref, out_ref, first, pairs, near, sums, held, far,
                  first_send, first_recv, near_send, near_recv, far_send, far_recv):
    me, row = lax.axis_index("col"), lax.axis_index("row")
    chip, core, chips = me // 2, me % 2, n // 2
    own, depth = out_ref.shape
    barrier = pltpu.get_barrier_semaphore()
    pl.semaphore_signal(barrier, inc=1, device_id=(row, chip * 2 + 1 - core), device_id_type=MESH)
    for step in range(1, chips):
        other = partner_of(chip, step, chips) * 2 + core
        pl.semaphore_signal(barrier, inc=1, device_id=(row, other), device_id_type=MESH)
    for step in range(1, m):
        pl.semaphore_signal(barrier, inc=1, device_id=(partner_of(row, step, m), me), device_id_type=MESH)
    pl.semaphore_wait(barrier, chips + m - 1)

    half = depth // 2 // LANES * LANES
    chunks = [slice(0, half), slice(half, depth)]

    def sibling(at, cols):
        return [pltpu.make_async_remote_copy(
            src_ref=part_ref.at[:, 1 - core, :, cols],
            dst_ref=first.at[:, :, cols],
            send_sem=first_send.at[at],
            recv_sem=first_recv.at[at],
            device_id=(row, chip * 2 + 1 - core),
            device_id_type=MESH,
        )]

    def plane(at, cols):
        copies = []
        for step in range(chips - 1, 0, -1):
            other = partner_of(chip, step, chips)
            copies.append(pltpu.make_async_remote_copy(
                src_ref=pairs.at[other, :, cols],
                dst_ref=near.at[step - 1, :, cols],
                send_sem=near_send.at[at, step - 1],
                recv_sem=near_recv.at[at, step - 1],
                device_id=(row, other * 2 + core),
                device_id_type=MESH,
            ))
        return copies

    def along(at, cols):
        copies = []
        for step in range(m - 1, 0, -1):
            other = partner_of(row, step, m)
            copies.append(pltpu.make_async_remote_copy(
                src_ref=held.at[other, :, cols],
                dst_ref=far.at[step - 1, :, cols],
                send_sem=far_send.at[at, step - 1],
                recv_sem=far_recv.at[at, step - 1],
                device_id=(other, me),
                device_id_type=MESH,
            ))
        return copies

    def start(copies):
        for copy in copies:
            copy.start()

    def wait(copies):
        for copy in copies:
            copy.wait()

    for at, cols in enumerate(chunks):
        start(sibling(at, cols))
    for at, cols in enumerate(chunks):
        wait(sibling(at, cols))
        for q in range(chips):
            both = part_ref[q, core, :, cols].astype(jnp.float32) + first[q, :, cols].astype(jnp.float32)
            pairs[q, :, cols] = both.astype(pairs.dtype)
        start(plane(at, cols))
    for at, cols in enumerate(chunks):
        wait(plane(at, cols))
        total = pairs[chip, :, cols].astype(jnp.float32)
        for step in range(1, chips):
            total = total + near[step - 1, :, cols].astype(jnp.float32)
        for r in range(m):
            sums[r, :, cols] = total[r * own:(r + 1) * own, :]
            held[r, :, cols] = total[r * own:(r + 1) * own, :].astype(held.dtype)
        start(along(at, cols))
    for at, cols in enumerate(chunks):
        wait(along(at, cols))
        total = sums[row, :, cols]
        for step in range(1, m):
            total = total + far[step - 1, :, cols].astype(jnp.float32)
        out_ref[:, cols] = total.astype(out_ref.dtype)


def reduce_scatter(part, n, m):
    count, depth = part.shape
    own, slab, chips = count // (n * m), count // n, n // 2
    vmem = pl.BlockSpec(memory_space=pltpu.VMEM)
    dma = pltpu.SemaphoreType.DMA
    return pl.pallas_call(
        functools.partial(reduce_kernel, n, m),
        out_shape=jax.ShapeDtypeStruct((own, depth), part.dtype),
        in_specs=[vmem],
        out_specs=vmem,
        scratch_shapes=[
            pltpu.VMEM((chips, slab, depth), part.dtype),
            pltpu.VMEM((chips, slab, depth), part.dtype),
            pltpu.VMEM((chips - 1, slab, depth), part.dtype),
            pltpu.VMEM((m, own, depth), jnp.float32),
            pltpu.VMEM((m, own, depth), part.dtype),
            pltpu.VMEM((m - 1, own, depth), part.dtype),
            dma((2,)), dma((2,)), dma((2, chips - 1)), dma((2, chips - 1)), dma((2, m - 1)), dma((2, m - 1)),
        ],
        compiler_params=pltpu.CompilerParams(
            collective_id=1, has_side_effects=True, vmem_limit_bytes=48 << 20
        ),
        name="reduce_scatter",
    )(part.reshape(chips, 2, slab, depth))


def body(joined_weight, tile_perm, down_weight, tokens, expert_ids, route_scores):
    n, m = lax.axis_size("col"), lax.axis_size("row")
    local, _, width = joined_weight.shape
    half = width // 2 // n
    tiles = tile_perm.shape[0]
    tile_cols = width // tiles
    places = jnp.arange(tiles, dtype=jnp.int32)
    inverse = jnp.sum(places[:, None] * (tile_perm[:, None] == places[None, :]), axis=0)
    first = inverse * tile_cols
    block = jnp.minimum(first // LANES, width // LANES - WINDOW // LANES)
    recv = exchange(joined_weight, block, first - block * LANES, n, half, tile_cols)
    everything = lax.all_gather(tokens, ("col", "row"), axis=0, tiled=True)
    base = lax.axis_index("row").astype(jnp.int32).reshape(1) * local
    own = tokens.shape[0]
    order = np.arange(m * n * own, dtype=np.int32).reshape(m, n, own).transpose(1, 0, 2).reshape(-1, 1)
    gate, up, part = experts(
        base, recv, everything, expert_ids.T, route_scores.T, jnp.asarray(order), down_weight
    )
    return jnp.swapaxes(gate, 1, 2), jnp.swapaxes(up, 1, 2), reduce_scatter(part, n, m)


def solution(mesh):
    placed = (P("row", "col", None), P(), P("row", "col", None), P(("row", "col"), None), P(), P())
    return jax.shard_map(
        body,
        mesh=mesh,
        in_specs=placed,
        out_specs=(P("row", None, "col"), P("row", None, "col"), P(("row", "col"), None)),
        check_vma=False,
    )
```

```python
import functools

import jax
import jax.numpy as jnp
import numpy as np
from jax import lax
from jax.experimental import pallas as pl
from jax.experimental.pallas import tpu as pltpu
from jax.sharding import PartitionSpec as P

MESH = pl.DeviceIdType.MESH
LANES = 128
WINDOW = 256
NT = (((1,), (1,)), ((), ()))


def partner_of(me, step, size):
    other = me
    bit = 1
    while bit < size:
        other = other + ((step // bit) % 2) * (1 - 2 * ((me // bit) % 2)) * bit
        bit *= 2
    return other


def block_plan(half, tile_cols):
    unit = tile_cols // 2
    plan, rows = [], []
    for first in range(0, half, LANES):
        units = first + np.arange(LANES)
        tiles = sorted(set((units[units < half] // unit).tolist()))
        at = []
        for tile in tiles:
            mine = (units // unit == tile) & (units < half)
            lane = np.where(mine, 2 * (units % unit), -(1 << 20))
            at.append(len(rows))
            rows.append(np.concatenate([lane, lane + 1]))
        plan.append((first, min(LANES, half - first), tiles, at))
    return plan, np.stack(rows, axis=1).astype(np.int32)


def pack_kernel(n, plan, tiles_each, start_ref, off_ref, lane_ref, joined_ref, recv_ref,
                held, send_buf, pick, send_sem, recv_sem, own_sem, load_sem):
    me, row = lax.axis_index("col"), lax.axis_index("row")
    local, blocks = joined_ref.shape[0], held.shape[0]

    def load_of(b):
        return pltpu.make_async_copy(
            joined_ref.at[:, :, b * LANES:(b + 1) * LANES], held.at[b], load_sem.at[b]
        )

    for b in range(blocks):
        load_of(b).start()
    barrier = pltpu.get_barrier_semaphore()
    for step in range(1, n):
        pl.semaphore_signal(barrier, inc=1, device_id=(row, partner_of(me, step, n)), device_id_type=MESH)
    pl.semaphore_wait(barrier, n - 1)

    def copy_of(turn, other):
        return pltpu.make_async_remote_copy(
            src_ref=send_buf.at[turn],
            dst_ref=recv_ref.at[me],
            send_sem=send_sem.at[turn],
            recv_sem=recv_sem.at[turn],
            device_id=(row, other),
            device_id_type=MESH,
        )

    def step_of(turn):
        return (n - 1) - (2 * turn) % (n - 1)

    def pack(turn, other):
        columns = lax.broadcasted_iota(jnp.int32, (2 * LANES, WINDOW), 1)
        for first, count, tiles, at in plan:
            starts = []
            for k, tile in enumerate(tiles):
                starts.append(start_ref[other * tiles_each + tile])
                off = off_ref[other * tiles_each + tile]
                wanted = lane_ref[:, at[k]:at[k] + 1] + off
                pick[:, k * WINDOW:(k + 1) * WINDOW] = jnp.where(columns == wanted, 1.0, 0.0).astype(pick.dtype)
            depth = len(tiles) * WINDOW
            for e in range(local):
                x = jnp.concatenate([held[s + w, e] for s in starts for w in range(WINDOW // LANES)], axis=1)
                y = lax.dot_general(pick[:, :depth], x, NT, preferred_element_type=jnp.float32)
                y = y.astype(send_buf.dtype)
                send_buf[turn, e, 0, first:first + count, :] = y[:count]
                send_buf[turn, e, 1, first:first + count, :] = y[LANES:LANES + count]

    def send(turn, carry):
        other = partner_of(me, step_of(turn), n)
        pack(turn, other)
        copy_of(turn, other).start()
        return carry

    for b in range(blocks):
        load_of(b).wait()
    lax.fori_loop(0, n - 1, send, 0)
    pack(n - 1, me)
    own = pltpu.make_async_copy(send_buf.at[n - 1], recv_ref.at[me], own_sem)
    own.start()

    def finish(turn, carry):
        copy_of(turn, partner_of(me, step_of(turn), n)).wait()
        return carry

    lax.fori_loop(0, n - 1, finish, 0)
    own.wait()


def exchange(joined_weight, start, off, n, half, tile_cols):
    local, rows, width = joined_weight.shape
    plan, lanes = block_plan(half, tile_cols)
    most = max(len(tiles) for _, _, tiles, _ in plan)
    smem = pl.BlockSpec(memory_space=pltpu.SMEM)
    vmem = pl.BlockSpec(memory_space=pltpu.VMEM)
    return pl.pallas_call(
        functools.partial(pack_kernel, n, plan, 2 * half // tile_cols),
        out_shape=jax.ShapeDtypeStruct((n, local, 2, half, rows), joined_weight.dtype),
        in_specs=[smem, smem, vmem, pl.BlockSpec(memory_space=pl.ANY)],
        out_specs=pl.BlockSpec(memory_space=pl.ANY),
        scratch_shapes=[
            pltpu.VMEM((width // LANES, local, rows, LANES), joined_weight.dtype),
            pltpu.VMEM((n, local, 2, half, rows), joined_weight.dtype),
            pltpu.VMEM((2 * LANES, most * WINDOW), joined_weight.dtype),
            pltpu.SemaphoreType.DMA((n - 1,)),
            pltpu.SemaphoreType.DMA((n - 1,)),
            pltpu.SemaphoreType.DMA,
            pltpu.SemaphoreType.DMA((width // LANES,)),
        ],
        compiler_params=pltpu.CompilerParams(
            collective_id=0, has_side_effects=True, vmem_limit_bytes=48 << 20
        ),
        cost_estimate=pl.CostEstimate(
            flops=2 * local * rows * WINDOW * 2 * width, bytes_accessed=4 * local * rows * width, transcendentals=0
        ),
        name="exchange",
    )(start, off, jnp.asarray(lanes), joined_weight)


def expert_kernel(n, base_ref, recv_ref, tok_ref, ids_ref, scores_ref, order_ref, down_ref,
                  gate_ref, up_ref, part_ref, total, both):
    e, part = pl.program_id(0), pl.program_id(1)
    begin = (e == 0) & (part == 0)
    last = (e == pl.num_programs(0) - 1) & (part == pl.num_programs(1) - 1)
    units, rows = recv_ref.shape[3:]
    second = both.shape[0] // 2
    for c in range(n):
        both[:units, c * rows:(c + 1) * rows] = recv_ref[c, 0, 0]
        both[second:second + units, c * rows:(c + 1) * rows] = recv_ref[c, 0, 1]
    gate_ref[0] = both[:units, :]
    up_ref[0] = both[second:second + units, :]
    scores = scores_ref[...]
    mine = jnp.where(ids_ref[...] == base_ref[0] + e, scores, 0.0)
    shares = jnp.sum(mine, axis=0, keepdims=True) / jnp.sum(scores, axis=0, keepdims=True)
    count = tok_ref.shape[0]
    source = lax.broadcasted_iota(jnp.int32, (count, count), 1)
    share = jnp.sum(jnp.where(source == order_ref[...], shares, 0.0), axis=1, keepdims=True)
    tokens = tok_ref[...]
    pre = lax.dot_general(tokens, both[...], NT, preferred_element_type=jnp.float32)
    pre_gate, pre_up = pre[:, :units], pre[:, second:second + units]
    active = share * (pre_up + 1.0) * pre_gate * jax.nn.sigmoid(1.702 * pre_gate)
    active = active.astype(down_ref.dtype)
    depth = down_ref.shape[2]
    for first in range(0, depth, 512):
        cols = slice(first, min(depth, first + 512))
        term = jnp.dot(active, down_ref[0, :, cols], preferred_element_type=jnp.float32)

        @pl.when(begin)
        def _():
            total[:, cols] = term

        @pl.when(jnp.logical_not(begin))
        def _():
            total[:, cols] += term

    @pl.when(last)
    def _():
        part_ref[...] = total[...].astype(part_ref.dtype)


def experts(base, recv, tokens, ids, scores, order, down_weight):
    n, local, _, _, rows = recv.shape
    half, depth = down_weight.shape[1:]
    count = tokens.shape[0]
    dtype = recv.dtype
    parts = 3 if half % 24 == 0 else 1
    units = half // parts
    return pl.pallas_call(
        functools.partial(expert_kernel, n),
        grid=(local, parts),
        out_shape=(
            jax.ShapeDtypeStruct((local, half, n * rows), dtype),
            jax.ShapeDtypeStruct((local, half, n * rows), dtype),
            jax.ShapeDtypeStruct((count, depth), dtype),
        ),
        in_specs=[
            pl.BlockSpec(memory_space=pltpu.SMEM),
            pl.BlockSpec((n, 1, 2, units, rows), lambda e, p: (0, e, 0, p, 0)),
            pl.BlockSpec((count, depth), lambda e, p: (0, 0)),
            pl.BlockSpec(ids.shape, lambda e, p: (0, 0)),
            pl.BlockSpec(scores.shape, lambda e, p: (0, 0)),
            pl.BlockSpec(order.shape, lambda e, p: (0, 0)),
            pl.BlockSpec((1, units, depth), lambda e, p: (e, p, 0)),
        ],
        out_specs=(
            pl.BlockSpec((1, units, n * rows), lambda e, p: (e, p, 0)),
            pl.BlockSpec((1, units, n * rows), lambda e, p: (e, p, 0)),
            pl.BlockSpec((count, depth), lambda e, p: (0, 0)),
        ),
        scratch_shapes=[
            pltpu.VMEM((count, depth), jnp.float32),
            pltpu.VMEM((2 * (-(-units // LANES) * LANES), n * rows), dtype),
        ],
        compiler_params=pltpu.CompilerParams(
            dimension_semantics=("arbitrary", "arbitrary"), vmem_limit_bytes=56 << 20
        ),
        name="experts",
    )(base, recv, tokens, ids, scores, order, down_weight)


def reduce_kernel(n, m, part_ref, out_ref, first, pairs, near, sums, held, far,
                  first_send, first_recv, near_send, near_recv, far_send, far_recv):
    me, row = lax.axis_index("col"), lax.axis_index("row")
    chip, core, chips = me // 2, me % 2, n // 2
    own, depth = out_ref.shape
    barrier = pltpu.get_barrier_semaphore()
    pl.semaphore_signal(barrier, inc=1, device_id=(row, chip * 2 + 1 - core), device_id_type=MESH)
    for step in range(1, chips):
        other = partner_of(chip, step, chips) * 2 + core
        pl.semaphore_signal(barrier, inc=1, device_id=(row, other), device_id_type=MESH)
    for step in range(1, m):
        pl.semaphore_signal(barrier, inc=1, device_id=(partner_of(row, step, m), me), device_id_type=MESH)
    pl.semaphore_wait(barrier, chips + m - 1)

    half = depth // 2 // LANES * LANES
    chunks = [slice(0, half), slice(half, depth)]

    def sibling(at, cols):
        return [pltpu.make_async_remote_copy(
            src_ref=part_ref.at[:, 1 - core, :, cols],
            dst_ref=first.at[:, :, cols],
            send_sem=first_send.at[at],
            recv_sem=first_recv.at[at],
            device_id=(row, chip * 2 + 1 - core),
            device_id_type=MESH,
        )]

    def plane(at, cols):
        copies = []
        for step in range(chips - 1, 0, -1):
            other = partner_of(chip, step, chips)
            copies.append(pltpu.make_async_remote_copy(
                src_ref=pairs.at[other, :, cols],
                dst_ref=near.at[step - 1, :, cols],
                send_sem=near_send.at[at, step - 1],
                recv_sem=near_recv.at[at, step - 1],
                device_id=(row, other * 2 + core),
                device_id_type=MESH,
            ))
        return copies

    def along(at, cols):
        copies = []
        for step in range(m - 1, 0, -1):
            other = partner_of(row, step, m)
            copies.append(pltpu.make_async_remote_copy(
                src_ref=held.at[other, :, cols],
                dst_ref=far.at[step - 1, :, cols],
                send_sem=far_send.at[at, step - 1],
                recv_sem=far_recv.at[at, step - 1],
                device_id=(other, me),
                device_id_type=MESH,
            ))
        return copies

    def start(copies):
        for copy in copies:
            copy.start()

    def wait(copies):
        for copy in copies:
            copy.wait()

    for at, cols in enumerate(chunks):
        start(sibling(at, cols))
    for at, cols in enumerate(chunks):
        wait(sibling(at, cols))
        for q in range(chips):
            both = part_ref[q, core, :, cols].astype(jnp.float32) + first[q, :, cols].astype(jnp.float32)
            pairs[q, :, cols] = both.astype(pairs.dtype)
        start(plane(at, cols))
    for at, cols in enumerate(chunks):
        wait(plane(at, cols))
        total = pairs[chip, :, cols].astype(jnp.float32)
        for step in range(1, chips):
            total = total + near[step - 1, :, cols].astype(jnp.float32)
        for r in range(m):
            sums[r, :, cols] = total[r * own:(r + 1) * own, :]
            held[r, :, cols] = total[r * own:(r + 1) * own, :].astype(held.dtype)
        start(along(at, cols))
    for at, cols in enumerate(chunks):
        wait(along(at, cols))
        total = sums[row, :, cols]
        for step in range(1, m):
            total = total + far[step - 1, :, cols].astype(jnp.float32)
        out_ref[:, cols] = total.astype(out_ref.dtype)


def reduce_scatter(part, n, m):
    count, depth = part.shape
    own, slab, chips = count // (n * m), count // n, n // 2
    vmem = pl.BlockSpec(memory_space=pltpu.VMEM)
    dma = pltpu.SemaphoreType.DMA
    return pl.pallas_call(
        functools.partial(reduce_kernel, n, m),
        out_shape=jax.ShapeDtypeStruct((own, depth), part.dtype),
        in_specs=[vmem],
        out_specs=vmem,
        scratch_shapes=[
            pltpu.VMEM((chips, slab, depth), part.dtype),
            pltpu.VMEM((chips, slab, depth), part.dtype),
            pltpu.VMEM((chips - 1, slab, depth), part.dtype),
            pltpu.VMEM((m, own, depth), jnp.float32),
            pltpu.VMEM((m, own, depth), part.dtype),
            pltpu.VMEM((m - 1, own, depth), part.dtype),
            dma((2,)), dma((2,)), dma((2, chips - 1)), dma((2, chips - 1)), dma((2, m - 1)), dma((2, m - 1)),
        ],
        compiler_params=pltpu.CompilerParams(
            collective_id=1, has_side_effects=True, vmem_limit_bytes=48 << 20
        ),
        name="reduce_scatter",
    )(part.reshape(chips, 2, slab, depth))


def body(joined_weight, tile_perm, down_weight, tokens, expert_ids, route_scores):
    n, m = lax.axis_size("col"), lax.axis_size("row")
    local, _, width = joined_weight.shape
    half = width // 2 // n
    tiles = tile_perm.shape[0]
    tile_cols = width // tiles
    places = jnp.arange(tiles, dtype=jnp.int32)
    inverse = jnp.sum(places[:, None] * (tile_perm[:, None] == places[None, :]), axis=0)
    first = inverse * tile_cols
    block = jnp.minimum(first // LANES, width // LANES - WINDOW // LANES)
    recv = exchange(joined_weight, block, first - block * LANES, n, half, tile_cols)
    everything = lax.all_gather(tokens, ("col", "row"), axis=0, tiled=True)
    base = lax.axis_index("row").astype(jnp.int32).reshape(1) * local
    own = tokens.shape[0]
    order = np.arange(m * n * own, dtype=np.int32).reshape(m, n, own).transpose(1, 0, 2).reshape(-1, 1)
    gate, up, part = experts(
        base, recv, everything, expert_ids.T, route_scores.T, jnp.asarray(order), down_weight
    )
    return jnp.swapaxes(gate, 1, 2), jnp.swapaxes(up, 1, 2), reduce_scatter(part, n, m)


def solution(mesh):
    placed = (P("row", "col", None), P(), P("row", "col", None), P(("row", "col"), None), P(), P())
    return jax.shard_map(
        body,
        mesh=mesh,
        in_specs=placed,
        out_specs=(P("row", None, "col"), P("row", None, "col"), P(("row", "col"), None)),
        check_vma=False,
    )
```
